512 devices in a mesh: comm: 64 (over x, y, core), blk: 8 (over z).
Axes of the slice: x: 4, y: 8, z: 8, core: 2. Of those that a mesh axis runs over, the one named last changes fastest.
Arguments:
- features: float32 [65536, 256], P(('comm', 'blk')), may hold values from -6 to 6
- tiles: float32 [65536, 1024], P(('comm', 'blk')), may hold values from -0.1875 to 0.1875
- weight: float32 [256, 256], replicated, may hold values from -0.375 to 0.375
- cotangent: float32 [65536, 256], P(('comm', 'blk')), may hold values from -6 to 6
- send_count: int32 [512, 64], P(('comm', 'blk')), may hold values from 0 to 16, as said below
- send_index: int32 [512, 1024], P(('comm', 'blk')), may hold values from 0 to 127
- cross_dst: int32 [512, 1024], P(('comm', 'blk')), may hold values from 0 to 127
- cross_weight: float32 [512, 1024], P(('comm', 'blk')), may hold values from -2.4 to 2.4
Outputs:
- output: float32 [65536, 256], P(('comm', 'blk'))
- grad_features: float32 [65536, 256], P(('comm', 'blk'))
- grad_weight: float32 [256, 256], replicated
The draws below stay inside these ranges and needn't reach their ends.
Inputs may be any that keep to these rules, and one draw needn't show every extreme that they name: send_count[d, p] is 0 where p is d's own community and at least 1 elsewhere; every device sends exactly 16 rows to some other community.
All inputs are finite; a program needn't handle non-finite values.
Results may differ from the reference program's by a relative error of at most 0.0003.
Values sent between devices are 32-bit elements; how exact they have to be, the bound alone decides.
A program may use at most 64 MiB of HBM per device.

```python
import jax
import jax.numpy as jnp
from jax import lax

ROWS = 128
H = 256
CAP = 16
NODES = 65536
BLOCK_COLS = 1024
SLOTS = 1024
N_COMM = 64
N_BLK = 8


def draw_send_count(key, part):
    key = jax.random.fold_in(key, 11)
    first, second = jax.random.split(key)
    senders = N_COMM * N_BLK
    counts = jax.random.randint(first, (senders, N_COMM), 1, CAP + 1)
    group = jnp.arange(senders, dtype=jnp.int32) // N_BLK
    full_peer = (group + 1 + jax.random.randint(second, (senders,), 0, N_COMM - 1)) % N_COMM
    peers = jnp.arange(N_COMM, dtype=jnp.int32)
    counts = jnp.where(peers[None, :] == full_peer[:, None], CAP, counts)
    counts = jnp.where(peers[None, :] == group[:, None], 0, counts)
    return counts.astype(jnp.int32)


def place_ends(entries, key, low, high):
    longest = entries.shape.index(max(entries.shape))
    spots = []
    for shift in (0, 1):
        where = [jax.random.randint(jax.random.fold_in(key, axis), (), 0, length) for axis, length in enumerate(entries.shape)]
        where[longest] = (where[longest] + shift) % entries.shape[longest]
        spots.append(tuple(where))
    return entries.at[spots[0]].set(low).at[spots[1]].set(high)


def steps_of(rng, extent, cuts, smallest, top_value):
    def one(dim, parts):
        heights = jax.random.uniform(jax.random.fold_in(jax.random.fold_in(rng, 6), dim), (parts,), jnp.float32, smallest / len(cuts), top_value / len(cuts))
        return jnp.repeat(jnp.exp(heights), extent[dim] // parts).reshape((-1,) + (1,) * (len(extent) - dim - 1))

    gain = one(*cuts[0])
    for cut in cuts[1:]:
        gain = gain * one(*cut)
    return gain


def gaussian(own_key, dims, deviation, bound, pieces=(), held_as=jnp.bfloat16):
    level = steps_of(own_key, dims, pieces, -0.22, 0.18) if pieces else 1.0
    values = jax.random.normal(own_key, dims, jnp.float32) * deviation * level
    return jnp.minimum(jnp.maximum(values, -bound), bound).astype(held_as)


def setup_inputs(seed: int = 0) -> dict:
    streams_of = jax.random.split(jax.random.key(seed), 9)
    features = gaussian(streams_of[0], (NODES, H), 1.0, 6.0, ((0, 512),), jnp.float32)
    tiles = gaussian(streams_of[1], (NODES, BLOCK_COLS), BLOCK_COLS ** -0.5, 0.1875, ((0, 512),), jnp.float32)
    weight = gaussian(streams_of[2], (H, H), H ** -0.5, 0.375, (), jnp.float32)
    cotangent = gaussian(streams_of[3], (NODES, H), 1.0, 6.0, ((0, 512),), jnp.float32)
    send_count = draw_send_count(jax.random.fold_in(streams_of[8], 71), 0)
    send_index = place_ends(jax.random.randint(streams_of[5], (N_COMM * N_BLK, SLOTS), 0, ROWS), jax.random.fold_in(streams_of[5], 1), 0, ROWS - 1).astype(jnp.int32)
    cross_dst = place_ends(jax.random.randint(streams_of[6], (N_COMM * N_BLK, SLOTS), 0, ROWS), jax.random.fold_in(streams_of[6], 1), 0, ROWS - 1).astype(jnp.int32)
    cross_weight = gaussian(streams_of[7], (N_COMM * N_BLK, SLOTS), 0.4, 2.4, ((0, 512),), jnp.float32)
    return {"features": features, "tiles": tiles, "weight": weight, "cotangent": cotangent, "send_count": send_count, "send_index": send_index, "cross_dst": cross_dst, "cross_weight": cross_weight}


def forward(features, weight, tiles, send_count, send_index, cross_dst, cross_weight):
    groups = N_COMM
    blocks = N_BLK
    grid = features.reshape(groups, blocks, ROWS, H)
    flat = features.reshape(groups, blocks * ROWS, H)
    tile_grid = tiles.reshape(groups, blocks, ROWS, blocks * ROWS)
    index = send_index.reshape(groups, blocks, groups, CAP)
    count = send_count.reshape(groups, blocks, groups)
    targets = cross_dst.reshape(groups, blocks, groups * CAP)
    edge_weight = cross_weight.reshape(groups, blocks, groups * CAP)
    slots = jnp.arange(CAP, dtype=jnp.int32)

    def one_group(group):
        local = jnp.einsum('brk,kh->brh', tile_grid[group], flat[group], precision=lax.Precision.HIGHEST)
        rows_in = index[:, :, group, :]
        picked = jax.vmap(jax.vmap(lambda table, where: table[where]))(grid, rows_in)
        valid = (slots[None, None, :] < count[:, :, group][:, :, None]).astype(jnp.float32)
        picked = picked * valid[:, :, :, None]
        received = jnp.transpose(picked, (1, 0, 2, 3)).reshape(blocks, groups * CAP, H)
        terms = edge_weight[group][:, :, None] * received
        cross = jax.vmap(lambda term, dest: jax.ops.segment_sum(term, dest, num_segments=ROWS))(terms, targets[group])
        return local + cross
    aggregated = lax.map(one_group, jnp.arange(groups, dtype=jnp.int32)).reshape(NODES, H)
    pre = jnp.dot(aggregated, weight, precision=lax.Precision.HIGHEST)
    return jax.nn.gelu(pre, approximate=False)

def reference(features, tiles, weight, cotangent, send_count, send_index, cross_dst, cross_weight):

    def layer(feature_in, weight_in):
        return forward(feature_in, weight_in, tiles, send_count, send_index, cross_dst, cross_weight)
    output, pull = jax.vjp(layer, features, weight)
    grad_features, grad_weight = pull(cotangent)
    return (output, grad_features, grad_weight * NODES ** (-0.5))
```

```python
import functools

import jax
import jax.numpy as jnp
from jax import lax
from jax.experimental import pallas as pl
from jax.experimental.pallas import tpu as pltpu
from jax.sharding import PartitionSpec as P

MESH = pl.DeviceIdType.MESH
F32 = jnp.float32
BF16 = jnp.bfloat16


def split(x):
    hi = x.astype(BF16)
    lo = (x - hi.astype(F32)).astype(BF16)
    return hi, lo


def mm(a, b, ca=1, cb=0):
    return lax.dot_general(a, b, (((ca,), (cb,)), ((), ())), preferred_element_type=F32)


def mm3(a, b, ca=1, cb=0):
    return mm(a[0], b[0], ca, cb) + (mm(a[0], b[1], ca, cb) + mm(a[1], b[0], ca, cb))


def kernel(
    groups, blocks, ny,
    f_ref, t_ref, w_ref, ct_ref, cnt_ref, idx_ref, dst_ref, cw_ref,
    out_ref, gf_ref, gw_ref,
    send_buf, recv_buf, gath, send2_buf, recv2_buf, part, part_in,
    wpart, wz, wa, wy, wfin, wall, wsum,
    sems,
):
    rows, width = f_ref.shape
    slots = idx_ref.shape[1]
    cap = slots // groups
    me_c = lax.axis_index("comm")
    me_b = lax.axis_index("blk")
    na = groups // ny
    core = lax.rem(me_c, 2)
    my_y = lax.rem(me_c // 2, ny)
    my_x = me_c // (2 * ny)
    my_a = my_x * 2 + core

    def a_peer(a):
        return ((a // 2) * ny + my_y) * 2 + lax.rem(a, 2)

    def y_peer(y):
        return (my_x * ny + y) * 2 + core

    barrier = pltpu.get_barrier_semaphore()

    @pl.loop(1, groups)
    def _(i):
        pl.semaphore_signal(barrier, inc=1, device_id=(lax.rem(me_c + i, groups), me_b), device_id_type=MESH)

    @pl.loop(1, blocks)
    def _(i):
        pl.semaphore_signal(barrier, inc=1, device_id=(me_c, lax.rem(me_b + i, blocks)), device_id_type=MESH)

    spot = lax.broadcasted_iota(jnp.int32, (groups, slots), 1) // cap
    peer = lax.broadcasted_iota(jnp.int32, (groups, slots), 0)
    expand = (spot == peer).astype(BF16)
    counts = jnp.broadcast_to(cnt_ref[...].astype(F32).astype(BF16), (16, groups))
    count = mm(counts, expand)[0:1, :]
    place = lax.rem(lax.broadcasted_iota(jnp.int32, (1, slots), 1), cap).astype(F32)
    index = jnp.where(place < count, idx_ref[...], -1)
    node = lax.broadcasted_iota(jnp.int32, (rows, slots), 0)
    pick = (node == index).astype(BF16)
    f = f_ref[...]
    f2 = split(f)
    send_buf[...] = mm(pick, f2[0], 0, 0) + mm(pick, f2[1], 0, 0)
    gath[pl.ds(pl.multiple_of(me_b * rows, rows), rows), :] = f
    own = pl.ds(pl.multiple_of(me_c * cap, cap), cap)
    recv_buf[own, :] = jnp.zeros((cap, width), F32)
    recv2_buf[own, :] = jnp.zeros((cap, width), F32)

    pl.semaphore_wait(barrier, groups + blocks - 2)

    def spread_comm(src, dst, s, r):
        @pl.loop(1, groups)
        def _(i):
            p = lax.rem(me_c + i, groups)
            pltpu.make_async_remote_copy(
                src_ref=src.at[pl.ds(pl.multiple_of(p * cap, cap), cap)],
                dst_ref=dst.at[own],
                send_sem=sems.at[s], recv_sem=sems.at[r],
                device_id=(p, me_b), device_id_type=MESH,
            ).start()

    def wait_bytes(ref, n, s):
        pltpu.make_async_copy(ref.at[pl.ds(0, n)], ref.at[pl.ds(0, n)], sems.at[s]).wait()

    @pl.loop(1, blocks)
    def _(i):
        pltpu.make_async_remote_copy(
            src_ref=f_ref,
            dst_ref=gath.at[pl.ds(pl.multiple_of(me_b * rows, rows), rows)],
            send_sem=sems.at[0], recv_sem=sems.at[1],
            device_id=(me_c, lax.rem(me_b + i, blocks)), device_id_type=MESH,
        ).start()

    spread_comm(send_buf, recv_buf, 2, 3)

    t2 = split(t_ref[...])
    feeds = node == dst_ref[...]
    cw2 = split(cw_ref[...])
    s2 = tuple(jnp.where(feeds, jnp.broadcast_to(c.astype(F32), (rows, slots)), 0.0).astype(BF16) for c in cw2)
    w2 = split(w_ref[...])

    wait_bytes(gath, rows * (blocks - 1), 1)
    agg = mm3(t2, split(gath[...]))
    wait_bytes(recv_buf, cap * (groups - 1), 3)
    agg = agg + mm3(s2, split(recv_buf[...]))
    agg2 = split(agg)
    pre = mm3(agg2, w2)
    cdf = 0.5 * (1.0 + lax.erf(pre * 0.7071067811865476))
    out_ref[...] = pre * cdf
    slope = cdf + pre * (jnp.exp(-0.5 * pre * pre) * 0.3989422804014327)
    gp = ct_ref[...] * slope
    gp2 = split(gp)
    wpart[...] = mm3(agg2, gp2, 0, 0)

    wrows = wpart.shape[0] // blocks

    @pl.loop(1, blocks)
    def _(i):
        j = lax.rem(me_b + i, blocks)
        pltpu.make_async_remote_copy(
            src_ref=wpart.at[pl.ds(pl.multiple_of(j * wrows, wrows), wrows)],
            dst_ref=wz.at[me_b],
            send_sem=sems.at[4], recv_sem=sems.at[5],
            device_id=(me_c, j), device_id_type=MESH,
        ).start()

    spread = mm3(gp2, w2, 1, 1)
    sp2 = split(spread)
    send2_buf[...] = mm3(s2, sp2, 0, 0)
    spread_comm(send2_buf, recv2_buf, 6, 7)
    part[...] = mm3(t2, sp2, 0, 0)

    @pl.loop(1, blocks)
    def _(i):
        j = lax.rem(me_b + i, blocks)
        pltpu.make_async_remote_copy(
            src_ref=part.at[pl.ds(pl.multiple_of(j * rows, rows), rows)],
            dst_ref=part_in.at[me_b],
            send_sem=sems.at[8], recv_sem=sems.at[9],
            device_id=(me_c, j), device_id_type=MESH,
        ).start()

    part_in[me_b] = part[pl.ds(pl.multiple_of(me_b * rows, rows), rows), :]

    wz[me_b] = wpart[pl.ds(pl.multiple_of(me_b * wrows, wrows), wrows), :]
    wait_bytes(wz, blocks - 1, 5)
    mine = jnp.sum(wz[...], axis=0)
    half = width // 2
    piece = 2 * wrows // na
    wsum[0:wrows, :] = mine[:, :half]
    wsum[wrows:, :] = mine[:, half:]

    @pl.loop(1, na)
    def _(i):
        a = lax.rem(my_a + i, na)
        pltpu.make_async_remote_copy(
            src_ref=wsum.at[pl.ds(pl.multiple_of(a * piece, piece), piece)],
            dst_ref=wa.at[my_a],
            send_sem=sems.at[10], recv_sem=sems.at[11],
            device_id=(a_peer(a), me_b), device_id_type=MESH,
        ).start()

    wa[my_a] = wsum[pl.ds(pl.multiple_of(my_a * piece, piece), piece), :]
    wait_bytes(wa, na - 1, 11)
    wy[my_y] = jnp.sum(wa[...], axis=0)

    @pl.loop(1, ny)
    def _(i):
        y = lax.rem(my_y + i, ny)
        pltpu.make_async_remote_copy(
            src_ref=wy.at[my_y],
            dst_ref=wy.at[my_y],
            send_sem=sems.at[12], recv_sem=sems.at[13],
            device_id=(y_peer(y), me_b), device_id_type=MESH,
        ).start()

    wait_bytes(wy, ny - 1, 13)
    nodes = rows * groups * blocks
    wfin[my_a] = jnp.sum(wy[...], axis=0) * nodes ** (-0.5)

    @pl.loop(1, na)
    def _(i):
        a = lax.rem(my_a + i, na)
        pltpu.make_async_remote_copy(
            src_ref=wfin.at[my_a],
            dst_ref=wfin.at[my_a],
            send_sem=sems.at[14], recv_sem=sems.at[15],
            device_id=(a_peer(a), me_b), device_id_type=MESH,
        ).start()

    wait_bytes(wfin, na - 1, 15)
    wall[me_b] = wfin[...].reshape(na * piece, half)

    @pl.loop(1, blocks)
    def _(i):
        j = lax.rem(me_b + i, blocks)
        pltpu.make_async_remote_copy(
            src_ref=wall.at[me_b],
            dst_ref=wall.at[me_b],
            send_sem=sems.at[16], recv_sem=sems.at[17],
            device_id=(me_c, j), device_id_type=MESH,
        ).start()

    wait_bytes(part_in, blocks - 1, 9)
    inner = jnp.sum(part_in[...], axis=0)
    wait_bytes(recv2_buf, cap * (groups - 1), 7)
    back2 = split(recv2_buf[...])
    gf_ref[...] = inner + (mm(pick, back2[0]) + mm(pick, back2[1]))

    wait_bytes(wall, blocks - 1, 17)
    for j in range(blocks):
        gw_ref[j * wrows:(j + 1) * wrows, :half] = wall[j, 0:wrows, :]
        gw_ref[j * wrows:(j + 1) * wrows, half:] = wall[j, wrows:, :]

    wait_bytes(gath, rows * (blocks - 1), 0)
    wait_bytes(recv_buf, cap * (groups - 1), 2)
    wait_bytes(wz, blocks - 1, 4)
    wait_bytes(recv2_buf, cap * (groups - 1), 6)
    wait_bytes(part_in, blocks - 1, 8)
    wait_bytes(wa, na - 1, 10)
    wait_bytes(wy, ny - 1, 12)
    wait_bytes(wfin, na - 1, 14)
    wait_bytes(wall, blocks - 1, 16)


def body(features, tiles, weight, cotangent, send_count, send_index, cross_dst, cross_weight):
    rows, width = features.shape
    groups = lax.axis_size("comm")
    blocks = lax.axis_size("blk")
    slots = send_index.shape[1]
    ny = 8
    na = groups // ny
    wrows = width // blocks
    piece = 2 * wrows // na
    half = width // 2
    vmem = pltpu.VMEM
    return pl.pallas_call(
        functools.partial(kernel, groups, blocks, ny),
        out_shape=(
            jax.ShapeDtypeStruct((rows, width), F32),
            jax.ShapeDtypeStruct((rows, width), F32),
            jax.ShapeDtypeStruct((width, width), F32),
        ),
        in_specs=[pl.BlockSpec(memory_space=vmem)] * 8,
        out_specs=(pl.BlockSpec(memory_space=vmem),) * 3,
        scratch_shapes=[
            vmem((slots, width), F32),
            vmem((slots, width), F32),
            vmem((blocks * rows, width), F32),
            vmem((slots, width), F32),
            vmem((slots, width), F32),
            vmem((blocks * rows, width), F32),
            vmem((blocks, rows, width), F32),
            vmem((width, width), F32),
            vmem((blocks, wrows, width), F32),
            vmem((na, piece, half), F32),
            vmem((ny, piece, half), F32),
            vmem((na, piece, half), F32),
            vmem((blocks, 2 * wrows, half), F32),
            vmem((2 * wrows, half), F32),
            pltpu.SemaphoreType.DMA((18,)),
        ],
        compiler_params=pltpu.CompilerParams(
            collective_id=0, has_side_effects=True, vmem_limit_bytes=40 * 1024 * 1024
        ),
    )(features, tiles, weight, cotangent, send_count, send_index, cross_dst, cross_weight)


def solution(mesh):
    rows = P(("comm", "blk"), None)
    return jax.shard_map(
        body,
        mesh=mesh,
        in_specs=(rows, rows, P(), rows, rows, rows, rows, rows),
        out_specs=(rows, rows, P()),
        check_vma=False,
    )
```

```python
import functools

import jax
import jax.numpy as jnp
from jax import lax
from jax.experimental import pallas as pl
from jax.experimental.pallas import tpu as pltpu
from jax.sharding import PartitionSpec as P

MESH = pl.DeviceIdType.MESH
F32 = jnp.float32
BF16 = jnp.bfloat16
NY = 8


def split(x):
    hi = x.astype(BF16)
    lo = (x - hi.astype(F32)).astype(BF16)
    return hi, lo


def mm(a, b, ca=1, cb=0):
    return lax.dot_general(a, b, (((ca,), (cb,)), ((), ())), preferred_element_type=F32)


def mm3(a, b, ca=1, cb=0):
    return mm(a[0], b[0], ca, cb) + (mm(a[0], b[1], ca, cb) + mm(a[1], b[0], ca, cb))


def at(i, n):
    return pl.ds(pl.multiple_of(i * n, n), n)


def kernel(
    groups, blocks,
    f_hbm, t_hbm, w_hbm, ct_hbm, cnt_hbm, idx_hbm, dst_hbm, cw_hbm,
    out_ref, gf_ref, gw_ref,
    t_ref, w_ref, ct_ref, cnt_ref, idx_ref, dst_ref, cw_ref,
    gath, picks, th, tl, idx_out, idx_in,
    send_buf, recv_buf, send2_buf, recv2_buf, part, rs_out, rs_in,
    wpart, wz, wa, wy, wfin, wall, wsum,
    loc, ag_r, ag_s, rs_r, rs_s, row_r, sems,
):
    rows, width = f_hbm.shape
    slots = idx_ref.shape[1]
    cap = slots // groups
    na = groups // NY
    unit = rows // 2
    me_c = lax.axis_index("comm")
    me_b = lax.axis_index("blk")
    core = lax.rem(me_c, 2)
    my_y = lax.rem(me_c // 2, NY)
    my_x = me_c // (2 * NY)
    my_a = my_x * 2 + core

    def a_dev(a):
        return (((a // 2) * NY + my_y) * 2 + lax.rem(a, 2), me_b)

    def y_dev(y):
        return ((my_x * NY + y) * 2 + core, me_b)

    def z_dev(z):
        return (me_c, z)

    ring = ((my_y, y_dev), (me_b, z_dev))
    n = NY

    def turn(r, d):
        return lax.rem(ring[r][0] + d + n, n)

    def send(src, dst, s, r, dev):
        pltpu.make_async_remote_copy(
            src_ref=src, dst_ref=dst, send_sem=s, recv_sem=r,
            device_id=dev, device_id_type=MESH,
        ).start()

    def wait_bytes(ref, s):
        pltpu.make_async_copy(ref, ref, s).wait()

    loads = [
        pltpu.make_async_copy(src, dst, loc.at[i])
        for i, (src, dst) in enumerate((
            (idx_hbm, idx_ref), (cnt_hbm, cnt_ref),
            (f_hbm, gath.at[0, at(my_y, rows)]), (f_hbm, gath.at[1, at(me_b, rows)]),
            (t_hbm, t_ref), (dst_hbm, dst_ref), (cw_hbm, cw_ref), (w_hbm, w_ref), (ct_hbm, ct_ref),
        ))
    ]
    for c in loads:
        c.start()

    barrier = pltpu.get_barrier_semaphore()

    @pl.loop(1, n)
    def _(i):
        pl.semaphore_signal(barrier, inc=1, device_id=y_dev(turn(0, i)), device_id_type=MESH)
        pl.semaphore_signal(barrier, inc=1, device_id=z_dev(turn(1, i)), device_id_type=MESH)
        pl.semaphore_signal(barrier, inc=1, device_id=a_dev(lax.rem(my_a + i, na)), device_id_type=MESH)

    per = na * cap
    spot = lax.broadcasted_iota(jnp.int32, (groups, slots), 1) // cap
    peer = lax.broadcasted_iota(jnp.int32, (groups, slots), 0)
    expand = (spot == peer).astype(BF16)
    lane = lax.broadcasted_iota(jnp.int32, (16, slots), 1)
    row16 = lax.broadcasted_iota(jnp.int32, (16, slots), 0)
    here = (lane // (2 * cap)) % NY == row16
    source = lax.broadcasted_iota(jnp.int32, (slots, per), 0)
    target = lax.broadcasted_iota(jnp.int32, (slots, per), 1)
    gather_lane = ((source // (2 * cap * NY)) * (2 * cap) + source % (2 * cap) == target).astype(BF16)
    loads[0].wait()
    loads[1].wait()
    counts = jnp.broadcast_to(cnt_ref[...].astype(F32).astype(BF16), (16, groups))
    count = mm(counts, expand)
    place = lax.rem(lane, cap).astype(F32)
    index = jnp.where(place < count, jnp.broadcast_to(idx_ref[...], (16, slots)).astype(F32), -1.0)
    mine = mm(jnp.where(here, index, 0.0).astype(BF16), gather_lane)
    for y in range(NY):
        idx_out[y] = jnp.broadcast_to(mine[y:y + 1, :], (8, per))
    idx_in[my_y] = idx_out[my_y]
    loads[2].wait()
    loads[3].wait()

    pl.semaphore_wait(barrier, 3 * (n - 1))

    def ag_slice(r, sign, u, origin):
        half = (u % 2) if sign > 0 else (1 - u % 2)
        return gath.at[r, pl.ds(pl.multiple_of(origin * rows + half * unit, unit), unit)]

    def ag_send(r, sign, u):
        origin = turn(r, -sign * (u // 2))
        s = ag_slice(r, sign, u, origin)
        k = 0 if sign > 0 else 1
        send(s, s, ag_s.at[2 * r + k], ag_r.at[(2 * r + k) * 7 + u], ring[r][1](turn(r, sign)))

    def ag_wait(r, sign, u):
        s = ag_slice(r, sign, u, turn(r, -sign * (u // 2 + 1)))
        k = 0 if sign > 0 else 1
        wait_bytes(s, ag_r.at[(2 * r + k) * 7 + u])

    @pl.loop(1, n)
    def _(i):
        y = turn(0, i)
        send(idx_out.at[y], idx_in.at[my_y], sems.at[0], sems.at[1], y_dev(y))

    for u in (0, 1):
        for r in (0, 1):
            for sign in (1, -1):
                ag_send(r, sign, u)

    node = lax.broadcasted_iota(jnp.int32, (rows, per), 0).astype(F32)

    def pick_block(y):
        pick = (node == idx_in[y][0:1, :]).astype(BF16)
        picks[y] = pick
        g = split(gath[0, at(y, rows), :])
        send_buf[y] = mm(pick, g[0], 0, 0) + mm(pick, g[1], 0, 0)
        there = at((my_x * NY + y) * 2 + core, cap)

        @pl.loop(1, na)
        def _(i):
            a = lax.rem(my_a + i, na)
            send(send_buf.at[y, at(a, cap)], recv_buf.at[there], sems.at[2], sems.at[3], a_dev(a))

        recv_buf[there, :] = send_buf[y, at(my_a, cap), :]

    pick_block(my_y)
    loads[4].wait()
    for j in range(blocks):
        hi, lo = split(t_ref[:, j * rows:(j + 1) * rows])
        th[j] = hi
        tl[j] = lo
    for c in loads[5:]:
        c.wait()
    feeds = lax.broadcasted_iota(jnp.int32, (rows, slots), 0) == dst_ref[...]
    s2 = tuple(
        jnp.where(feeds, jnp.broadcast_to(c.astype(F32), (rows, slots)), 0.0).astype(BF16)
        for c in split(cw_ref[...])
    )
    w2 = split(w_ref[...])

    def local_block(j):
        return mm3((th[j], tl[j]), split(gath[1, at(j, rows), :]))

    agg = local_block(me_b)
    wait_bytes(idx_in.at[pl.ds(0, n - 1)], sems.at[1])
    for d in (1, 2, 3):
        for h in (0, 1):
            u = 2 * (d - 1) + h
            for r in (0, 1):
                for sign in (1, -1):
                    ag_wait(r, sign, u)
                    if u < 5:
                        ag_send(r, sign, u + 2)
        pick_block(turn(0, d))
        pick_block(turn(0, -d))
        agg = agg + local_block(turn(1, d)) + local_block(turn(1, -d))
    for r in (0, 1):
        for sign in (1, -1):
            ag_wait(r, sign, 6)
    pick_block(turn(0, 4))
    agg = agg + local_block(turn(1, 4))

    wait_bytes(recv_buf.at[pl.ds(0, cap * n * (na - 1))], sems.at[3])
    agg = agg + mm3(s2, split(recv_buf[...]))
    agg2 = split(agg)
    pre = mm3(agg2, w2)
    cdf = 0.5 * (1.0 + lax.erf(pre * 0.7071067811865476))
    out_ref[...] = pre * cdf
    slope = cdf + pre * (jnp.exp(-0.5 * pre * pre) * 0.3989422804014327)
    gp2 = split(ct_ref[...] * slope)

    sp2 = split(mm3(gp2, w2, 1, 1))
    send2_buf[...] = mm3(s2, sp2, 0, 0)

    def give_back(y):
        @pl.loop(1, na)
        def _(i):
            a = lax.rem(my_a + i, na)
            p = ((a // 2) * NY + y) * 2 + lax.rem(a, 2)
            send(send2_buf.at[at(p, cap)], recv2_buf.at[y, at(my_a, cap)], sems.at[4], row_r.at[y], a_dev(a))

        recv2_buf[y, at(my_a, cap), :] = send2_buf[at((my_x * NY + y) * 2 + core, cap), :]

    for d in (4, 3, -3, 2, -2, 1, -1, 0):
        give_back(turn(0, d))

    wpart[...] = mm3(agg2, gp2, 0, 0)
    wrows = wpart.shape[0] // blocks

    @pl.loop(1, blocks)
    def _(i):
        j = turn(1, i)
        send(wpart.at[at(j, wrows)], wz.at[me_b], sems.at[6], sems.at[7], z_dev(j))

    wz[me_b] = wpart[at(me_b, wrows), :]

    for j in range(blocks):
        part[1, j] = mm3((th[j], tl[j]), sp2, 0, 0)

    def boundary_block(y):
        wait_bytes(recv2_buf.at[y, pl.ds(0, cap * (na - 1))], row_r.at[y])
        b = split(recv2_buf[y])
        part[0, y] = mm(picks[y], b[0]) + mm(picks[y], b[1])

    def rs_half(sign, u):
        return (u % 2) if sign > 0 else (1 - u % 2)

    def rs_step(r, sign, u):
        k = 2 * r + (0 if sign > 0 else 1)
        owner = turn(r, sign * (4 - (u + 1) // 2))
        h = rs_half(sign, u) * unit
        v = part[r, owner, h:h + unit, :]
        if u >= 2:
            wait_bytes(rs_in.at[k, u - 2], rs_r.at[k * 7 + u - 2])
            v = v + rs_in[k, u - 2]
        rs_out[k, u] = v
        send(rs_out.at[k, u], rs_in.at[k, u], rs_s.at[k], rs_r.at[k * 7 + u], ring[r][1](turn(r, sign)))

    def rs_all(r, u):
        rs_step(r, 1, u)
        rs_step(r, -1, u)

    rs_all(1, 0)
    rs_all(1, 1)
    boundary_block(turn(0, 4))
    rs_all(0, 0)
    boundary_block(turn(0, 3))
    boundary_block(turn(0, -3))
    rs_all(0, 1)

    half = width // 2
    piece = 2 * wrows // na

    def weight_a():
        wait_bytes(wz.at[pl.ds(0, blocks - 1)], sems.at[7])
        total = jnp.sum(wz[...], axis=0)
        wsum[0:wrows, :] = total[:, :half]
        wsum[wrows:, :] = total[:, half:]

        @pl.loop(1, na)
        def _(i):
            a = lax.rem(my_a + i, na)
            send(wsum.at[at(a, piece)], wa.at[my_a], sems.at[8], sems.at[9], a_dev(a))

        wa[my_a] = wsum[at(my_a, piece), :]

    def weight_y():
        wait_bytes(wa.at[pl.ds(0, na - 1)], sems.at[9])
        wy[my_y] = jnp.sum(wa[...], axis=0)

        @pl.loop(1, n)
        def _(i):
            send(wy.at[my_y], wy.at[my_y], sems.at[10], sems.at[11], y_dev(turn(0, i)))

    def weight_back_a():
        wait_bytes(wy.at[pl.ds(0, n - 1)], sems.at[11])
        nodes = rows * groups * blocks
        wfin[my_a] = jnp.sum(wy[...], axis=0) * nodes ** (-0.5)

        @pl.loop(1, na)
        def _(i):
            send(wfin.at[my_a], wfin.at[my_a], sems.at[12], sems.at[13], a_dev(lax.rem(my_a + i, na)))

    def weight_back_z():
        wait_bytes(wfin.at[pl.ds(0, na - 1)], sems.at[13])
        wall[me_b] = wfin[...].reshape(na * piece, half)

        @pl.loop(1, blocks)
        def _(i):
            send(wall.at[me_b], wall.at[me_b], sems.at[14], sems.at[15], z_dev(turn(1, i)))

    rs_all(1, 2)
    rs_all(0, 2)
    weight_a()
    boundary_block(turn(0, 2))
    boundary_block(turn(0, -2))
    rs_all(1, 3)
    rs_all(0, 3)
    weight_y()
    rs_all(1, 4)
    rs_all(0, 4)
    weight_back_a()
    boundary_block(turn(0, 1))
    boundary_block(turn(0, -1))
    rs_all(1, 5)
    rs_all(0, 5)
    weight_back_z()
    rs_all(1, 6)
    rs_all(0, 6)
    boundary_block(my_y)

    for r in (0, 1):
        for u in (5, 6):
            for k in (2 * r, 2 * r + 1):
                wait_bytes(rs_in.at[k, u], rs_r.at[k * 7 + u])
    for h in (0, 1):
        own = part[0, my_y, h * unit:(h + 1) * unit, :] + part[1, me_b, h * unit:(h + 1) * unit, :]
        for r in (0, 1):
            own = own + (rs_in[2 * r, 6 - h] + rs_in[2 * r + 1, 5 + h])
        gf_ref[h * unit:(h + 1) * unit, :] = own

    wait_bytes(wall.at[pl.ds(0, blocks - 1)], sems.at[15])
    for j in range(blocks):
        gw_ref[j * wrows:(j + 1) * wrows, :half] = wall[j, 0:wrows, :]
        gw_ref[j * wrows:(j + 1) * wrows, half:] = wall[j, wrows:, :]

    for k in range(4):
        wait_bytes(gath.at[0, pl.ds(0, 7 * unit)], ag_s.at[k])
        wait_bytes(rs_out.at[k], rs_s.at[k])
    wait_bytes(idx_out.at[pl.ds(0, n - 1)], sems.at[0])
    wait_bytes(recv_buf.at[pl.ds(0, cap * n * (na - 1))], sems.at[2])
    wait_bytes(recv_buf.at[pl.ds(0, cap * n * (na - 1))], sems.at[4])
    wait_bytes(wz.at[pl.ds(0, blocks - 1)], sems.at[6])
    wait_bytes(wa.at[pl.ds(0, na - 1)], sems.at[8])
    wait_bytes(wy.at[pl.ds(0, n - 1)], sems.at[10])
    wait_bytes(wfin.at[pl.ds(0, na - 1)], sems.at[12])
    wait_bytes(wall.at[pl.ds(0, blocks - 1)], sems.at[14])


def body(features, tiles, weight, cotangent, send_count, send_index, cross_dst, cross_weight):
    rows, width = features.shape
    groups = lax.axis_size("comm")
    blocks = lax.axis_size("blk")
    slots = send_index.shape[1]
    cap = slots // groups
    na = groups // NY
    per = na * cap
    unit = rows // 2
    wrows = width // blocks
    piece = 2 * wrows // na
    half = width // 2
    vmem = pltpu.VMEM
    dma = pltpu.SemaphoreType.DMA
    return pl.pallas_call(
        functools.partial(kernel, groups, blocks),
        out_shape=(
            jax.ShapeDtypeStruct((rows, width), F32),
            jax.ShapeDtypeStruct((rows, width), F32),
            jax.ShapeDtypeStruct((width, width), F32),
        ),
        in_specs=[pl.BlockSpec(memory_space=pltpu.HBM)] * 8,
        out_specs=(pl.BlockSpec(memory_space=vmem),) * 3,
        scratch_shapes=[
            vmem(tiles.shape, F32), vmem(weight.shape, F32), vmem((rows, width), F32),
            vmem(send_count.shape, jnp.int32), vmem(send_index.shape, jnp.int32),
            vmem(cross_dst.shape, jnp.int32), vmem(cross_weight.shape, F32),
            vmem((2, NY * rows, width), F32),
            vmem((NY, rows, per), BF16),
            vmem((blocks, rows, rows), BF16), vmem((blocks, rows, rows), BF16),
            vmem((NY, 8, per), F32), vmem((NY, 8, per), F32),
            vmem((NY, per, width), F32), vmem((slots, width), F32),
            vmem((slots, width), F32), vmem((NY, per, width), F32),
            vmem((2, NY, rows, width), F32),
            vmem((4, 7, unit, width), F32), vmem((4, 7, unit, width), F32),
            vmem((width, width), F32),
            vmem((blocks, wrows, width), F32),
            vmem((na, piece, half), F32),
            vmem((NY, piece, half), F32),
            vmem((na, piece, half), F32),
            vmem((blocks, 2 * wrows, half), F32),
            vmem((2 * wrows, half), F32),
            dma((9,)), dma((28,)), dma((4,)), dma((28,)), dma((4,)), dma((NY,)), dma((16,)),
        ],
        compiler_params=pltpu.CompilerParams(
            collective_id=0, has_side_effects=True, vmem_limit_bytes=60 * 1024 * 1024
        ),
    )(features, tiles, weight, cotangent, send_count, send_index, cross_dst, cross_weight)


def solution(mesh):
    rows = P(("comm", "blk"), None)
    return jax.shard_map(
        body,
        mesh=mesh,
        in_specs=(rows, rows, P(), rows, rows, rows, rows, rows),
        out_specs=(rows, rows, P()),
        check_vma=False,
    )
```

```python
import functools

import jax
import jax.numpy as jnp
from jax import lax
from jax.experimental import pallas as pl
from jax.experimental.pallas import tpu as pltpu
from jax.sharding import PartitionSpec as P

MESH = pl.DeviceIdType.MESH
F32 = jnp.float32
BF16 = jnp.bfloat16
NY = 8
PARTS = 4
UNITS = 7 * PARTS // 2


def split(x):
    hi = x.astype(BF16)
    lo = (x - hi.astype(F32)).astype(BF16)
    return hi, lo


def mm(a, b, ca=1, cb=0):
    return lax.dot_general(a, b, (((ca,), (cb,)), ((), ())), preferred_element_type=F32)


def left(x, axis=1):
    return jnp.concatenate((x[0], x[0], x[1]), axis=axis)


def right(x):
    return jnp.concatenate((x[0], x[1], x[0]), axis=0)


def at(i, n):
    return pl.ds(pl.multiple_of(i * n, n), n)


def kernel(
    groups, blocks,
    f_hbm, t_hbm, w_hbm, ct_hbm, cnt_hbm, idx_hbm, dst_hbm, cw_hbm,
    out_ref, gf_ref, gw_ref,
    t_ref, w_ref, ct_ref, cnt_ref, idx_ref, dst_ref, cw_ref,
    gath, picks, t3, tt3, s3, st3, w3, wt3, idx_out, idx_in,
    send_buf, recv_buf, send2_buf, recv2_buf, part, rs_out, rs_in,
    wpart, wz, wa, wy, wfin, wall, wsum,
    loc, ag_r, ag_s, rs_r, rs_s, row_r, rowf_r, sems,
):
    rows, width = f_hbm.shape
    slots = idx_ref.shape[1]
    cap = slots // groups
    na = groups // NY
    unit = rows // PARTS
    me_c = lax.axis_index("comm")
    me_b = lax.axis_index("blk")
    core = lax.rem(me_c, 2)
    my_y = lax.rem(me_c // 2, NY)
    my_x = me_c // (2 * NY)
    my_a = my_x * 2 + core

    def a_dev(a):
        return (((a // 2) * NY + my_y) * 2 + lax.rem(a, 2), me_b)

    def y_dev(y):
        return ((my_x * NY + y) * 2 + core, me_b)

    def z_dev(z):
        return (me_c, z)

    ring = ((my_y, y_dev), (me_b, z_dev))
    n = NY

    def turn(r, d):
        return lax.rem(ring[r][0] + d + n, n)

    def send(src, dst, s, r, dev):
        pltpu.make_async_remote_copy(
            src_ref=src, dst_ref=dst, send_sem=s, recv_sem=r,
            device_id=dev, device_id_type=MESH,
        ).start()

    def wait_bytes(ref, s):
        pltpu.make_async_copy(ref, ref, s).wait()

    loads = [
        pltpu.make_async_copy(src, dst, loc.at[i])
        for i, (src, dst) in enumerate((
            (idx_hbm, idx_ref), (cnt_hbm, cnt_ref),
            (f_hbm, gath.at[0, at(my_y, rows)]), (f_hbm, gath.at[1, at(me_b, rows)]),
            (t_hbm, t_ref), (dst_hbm, dst_ref), (cw_hbm, cw_ref), (w_hbm, w_ref), (ct_hbm, ct_ref),
        ))
    ]
    for c in loads:
        c.start()

    barrier = pltpu.get_barrier_semaphore()

    @pl.loop(1, n)
    def _(i):
        pl.semaphore_signal(barrier, inc=1, device_id=y_dev(turn(0, i)), device_id_type=MESH)
        pl.semaphore_signal(barrier, inc=1, device_id=z_dev(turn(1, i)), device_id_type=MESH)
        pl.semaphore_signal(barrier, inc=1, device_id=a_dev(lax.rem(my_a + i, na)), device_id_type=MESH)

    loads[2].wait()
    loads[3].wait()

    pl.semaphore_wait(barrier, 3 * (n - 1))

    def part_of(sign, u):
        return (u % PARTS) if sign > 0 else (PARTS - 1 - u % PARTS)

    def ring_no(r, sign):
        return 2 * r + (0 if sign > 0 else 1)

    def ag_slice(r, sign, u, origin):
        return gath.at[r, pl.ds(pl.multiple_of(origin * rows + part_of(sign, u) * unit, unit), unit)]

    def ag_send(r, sign, u):
        s = ag_slice(r, sign, u, turn(r, -sign * (u // PARTS)))
        k = ring_no(r, sign)
        send(s, s, ag_s.at[k], ag_r.at[k * UNITS + u], ring[r][1](turn(r, sign)))

    def ag_wait(r, sign, u):
        s = ag_slice(r, sign, u, turn(r, -sign * (u // PARTS + 1)))
        wait_bytes(s, ag_r.at[ring_no(r, sign) * UNITS + u])

    for u in range(PARTS):
        for r in (0, 1):
            for sign in (1, -1):
                ag_send(r, sign, u)

    per = na * cap
    spot = lax.broadcasted_iota(jnp.int32, (groups, slots), 1) // cap
    peer = lax.broadcasted_iota(jnp.int32, (groups, slots), 0)
    expand = (spot == peer).astype(BF16)
    lane = lax.broadcasted_iota(jnp.int32, (16, slots), 1)
    row16 = lax.broadcasted_iota(jnp.int32, (16, slots), 0)
    here = (lane // (2 * cap)) % NY == row16
    source = lax.broadcasted_iota(jnp.int32, (slots, per), 0)
    target = lax.broadcasted_iota(jnp.int32, (slots, per), 1)
    gather_lane = ((source // (2 * cap * NY)) * (2 * cap) + source % (2 * cap) == target).astype(BF16)
    place = lax.rem(lane, cap).astype(F32)

    def by_y(v):
        v = jnp.broadcast_to(v, (16, slots)).astype(F32)
        return mm(jnp.where(here, v, 0.0).astype(BF16), gather_lane)

    loads[0].wait()
    loads[1].wait()
    counts = jnp.broadcast_to(cnt_ref[...].astype(F32).astype(BF16), (16, groups))
    count = mm(counts, expand)
    index = jnp.where(place < count, jnp.broadcast_to(idx_ref[...], (16, slots)).astype(F32), -1.0)
    mine = by_y(index)
    for y in range(NY):
        idx_out[y] = jnp.broadcast_to(mine[y:y + 1, :], (8, per))
    idx_in[my_y] = idx_out[my_y]

    @pl.loop(1, n)
    def _(i):
        y = turn(0, i)
        send(idx_out.at[y], idx_in.at[my_y], sems.at[0], sems.at[1], y_dev(y))

    node = lax.broadcasted_iota(jnp.int32, (rows, per), 0).astype(F32)

    def pick_block(y):
        pick = (node == idx_in[y][0:1, :]).astype(F32)
        one = pick.astype(BF16)
        picks[y] = jnp.concatenate((one, one), axis=1)
        flip = pick.T.astype(BF16)
        g = split(gath[0, at(y, rows), :])
        send_buf[y] = mm(jnp.concatenate((flip, flip), axis=1), jnp.concatenate(g, axis=0))

        @pl.loop(1, na)
        def _(i):
            a = lax.rem(my_a + i, na)
            send(send_buf.at[y, at(a, cap)], recv_buf.at[y, at(my_a, cap)], sems.at[2], rowf_r.at[y], a_dev(a))

        recv_buf[y, at(my_a, cap), :] = send_buf[y, at(my_a, cap), :]

    def make_tiles(js):
        for j in js:
            v = t_ref[:, j * rows:(j + 1) * rows]
            t3[j] = left(split(v))
            tt3[j] = left(split(v.T))

    def cross_wait(y):
        wait_bytes(recv_buf.at[y, pl.ds(0, cap * (na - 1))], rowf_r.at[y])

    def gathered(ref, blocks_of, data):
        a = jnp.concatenate([ref[b] for b in blocks_of], axis=1)
        return mm(a, jnp.concatenate([right(split(data(b))) for b in blocks_of], axis=0))

    def local_blocks(*js):
        return gathered(t3, js, lambda j: gath[1, at(j, rows), :])

    def cross_blocks(*ys):
        for y in ys:
            cross_wait(y)
        return gathered(s3, ys, lambda y: recv_buf[y])

    def ring_step(k):
        for u in range(k * PARTS // 2, (k + 1) * PARTS // 2):
            for r in (0, 1):
                for sign in (1, -1):
                    ag_wait(r, sign, u)
                    if u + PARTS < UNITS:
                        ag_send(r, sign, u + PARTS)

    pick_block(my_y)
    ring_step(0)
    for c in loads[4:]:
        c.wait()
    make_tiles(range(blocks))
    wait_bytes(idx_in.at[pl.ds(0, n - 1)], sems.at[1])
    ring_step(1)
    pick_block(turn(0, 1))
    pick_block(turn(0, -1))
    ring_step(2)
    feed = by_y(dst_ref[...])
    cw2 = split(cw_ref[...])
    weight_hi = by_y(cw2[0].astype(F32))
    weight_lo = by_y(cw2[1].astype(F32))
    for y in range(NY):
        hit = node == feed[y:y + 1, :]
        hi = jnp.where(hit, jnp.broadcast_to(weight_hi[y:y + 1, :], (rows, per)), 0.0)
        lo = jnp.where(hit, jnp.broadcast_to(weight_lo[y:y + 1, :], (rows, per)), 0.0)
        s3[y] = left((hi.astype(BF16), lo.astype(BF16)))
        st3[y] = left((hi.T.astype(BF16), lo.T.astype(BF16)))
    ring_step(3)
    pick_block(turn(0, 2))
    pick_block(turn(0, -2))
    ring_step(4)
    w3[...] = right(split(w_ref[...]))
    wt3[...] = right(split(w_ref[...].T))
    agg = local_blocks(me_b, turn(1, 1), turn(1, -1))
    ring_step(5)
    pick_block(turn(0, 3))
    pick_block(turn(0, -3))
    ring_step(6)
    pick_block(turn(0, 4))
    agg = agg + local_blocks(turn(1, 2), turn(1, -2))
    agg = agg + local_blocks(turn(1, 3), turn(1, -3), turn(1, 4))
    agg = agg + cross_blocks(my_y, turn(0, 1), turn(0, -1))
    agg = agg + cross_blocks(turn(0, 2), turn(0, -2))
    agg = agg + cross_blocks(turn(0, 3), turn(0, -3), turn(0, 4))
    agg2 = split(agg)
    pre = mm(left(agg2), w3[...])
    cdf = 0.5 * (1.0 + lax.erf(pre * 0.7071067811865476))
    out_ref[...] = pre * cdf
    slope = cdf + pre * (jnp.exp(-0.5 * pre * pre) * 0.3989422804014327)
    gp2 = split(ct_ref[...] * slope)

    sp3 = right(split(mm(left(gp2), wt3[...])))

    def give_back(y):
        send2_buf[y] = mm(st3[y], sp3)

        @pl.loop(1, na)
        def _(i):
            a = lax.rem(my_a + i, na)
            send(send2_buf.at[y, at(a, cap)], recv2_buf.at[y, at(my_a, cap)], sems.at[4], row_r.at[y], a_dev(a))

        recv2_buf[y, at(my_a, cap), :] = send2_buf[y, at(my_a, cap), :]

    def inner_block(j):
        part[1, j] = mm(tt3[j], sp3)

    def boundary_block(y):
        wait_bytes(recv2_buf.at[y, pl.ds(0, cap * (na - 1))], row_r.at[y])
        part[0, y] = mm(picks[y], jnp.concatenate(split(recv2_buf[y]), axis=0))

    def rs_step(r, sign, u):
        k = ring_no(r, sign)
        owner = turn(r, sign * (4 - (u + PARTS // 2) // PARTS))
        h = part_of(sign, u) * unit
        v = part[r, owner, h:h + unit, :]
        if u >= PARTS:
            wait_bytes(rs_in.at[k, u - PARTS], rs_r.at[k * UNITS + u - PARTS])
            v = v + rs_in[k, u - PARTS]
        rs_out[k, u] = v
        send(rs_out.at[k, u], rs_in.at[k, u], rs_s.at[k], rs_r.at[k * UNITS + u], ring[r][1](turn(r, sign)))

    def rs_all(r, k):
        for u in range(k * PARTS // 2, (k + 1) * PARTS // 2):
            rs_step(r, 1, u)
            rs_step(r, -1, u)

    wrows = width // na
    half = width // 2
    piece = 2 * wrows // n

    def weight_1():
        wpart[...] = mm(left(agg2, 0), right(gp2), 0, 0)

        @pl.loop(1, na)
        def _(i):
            a = lax.rem(my_a + i, na)
            send(wpart.at[at(a, wrows)], wz.at[my_a], sems.at[6], sems.at[7], a_dev(a))

        wz[my_a] = wpart[at(my_a, wrows), :]

    def weight_2():
        wait_bytes(wz.at[pl.ds(0, na - 1)], sems.at[7])
        total = jnp.sum(wz[...], axis=0)
        wsum[0:wrows, :] = total[:, :half]
        wsum[wrows:, :] = total[:, half:]

        @pl.loop(1, n)
        def _(i):
            y = turn(0, i)
            send(wsum.at[at(y, piece)], wa.at[my_y], sems.at[8], sems.at[9], y_dev(y))

        wa[my_y] = wsum[at(my_y, piece), :]

    def weight_3():
        wait_bytes(wa.at[pl.ds(0, n - 1)], sems.at[9])
        wy[me_b] = jnp.sum(wa[...], axis=0)

        @pl.loop(1, n)
        def _(i):
            send(wy.at[me_b], wy.at[me_b], sems.at[10], sems.at[11], z_dev(turn(1, i)))

    def weight_4():
        wait_bytes(wy.at[pl.ds(0, n - 1)], sems.at[11])
        nodes = rows * groups * blocks
        wfin[my_y] = jnp.sum(wy[...], axis=0) * nodes ** (-0.5)

        @pl.loop(1, n)
        def _(i):
            send(wfin.at[my_y], wfin.at[my_y], sems.at[12], sems.at[13], y_dev(turn(0, i)))

    def weight_5():
        wait_bytes(wfin.at[pl.ds(0, n - 1)], sems.at[13])
        wall[my_a] = wfin[...].reshape(n * piece, half)

        @pl.loop(1, na)
        def _(i):
            send(wall.at[my_a], wall.at[my_a], sems.at[14], sems.at[15], a_dev(lax.rem(my_a + i, na)))

    weight_1()
    inner_block(turn(1, 4))
    rs_all(1, 0)
    inner_block(turn(1, 3))
    inner_block(turn(1, -3))
    rs_all(1, 1)
    for d in (4, 3, -3, 2, -2, 1, -1, 0):
        give_back(turn(0, d))
    inner_block(turn(1, 2))
    inner_block(turn(1, -2))
    rs_all(1, 2)
    weight_2()
    boundary_block(turn(0, 4))
    rs_all(0, 0)
    boundary_block(turn(0, 3))
    boundary_block(turn(0, -3))
    rs_all(0, 1)
    rs_all(1, 3)
    inner_block(turn(1, 1))
    inner_block(turn(1, -1))
    weight_3()
    rs_all(1, 4)
    rs_all(0, 2)
    boundary_block(turn(0, 2))
    boundary_block(turn(0, -2))
    rs_all(0, 3)
    weight_4()
    rs_all(1, 5)
    rs_all(0, 4)
    boundary_block(turn(0, 1))
    boundary_block(turn(0, -1))
    rs_all(0, 5)
    rs_all(1, 6)
    weight_5()
    rs_all(0, 6)
    inner_block(me_b)
    boundary_block(my_y)

    last = range(UNITS - PARTS, UNITS)
    for k in range(4):
        for u in last:
            wait_bytes(rs_in.at[k, u], rs_r.at[k * UNITS + u])
    for h in range(PARTS):
        at_h = slice(h * unit, (h + 1) * unit)
        own = part[0, my_y, at_h, :] + part[1, me_b, at_h, :]
        for r in (0, 1):
            for sign in (1, -1):
                for u in last:
                    if part_of(sign, u) == h:
                        own = own + rs_in[ring_no(r, sign), u]
        gf_ref[at_h, :] = own

    wait_bytes(wall.at[pl.ds(0, na - 1)], sems.at[15])
    for j in range(na):
        gw_ref[j * wrows:(j + 1) * wrows, :half] = wall[j, 0:wrows, :]
        gw_ref[j * wrows:(j + 1) * wrows, half:] = wall[j, wrows:, :]

    for k in range(4):
        wait_bytes(gath.at[0, pl.ds(0, UNITS * unit)], ag_s.at[k])
        wait_bytes(rs_out.at[k], rs_s.at[k])
    wait_bytes(idx_out.at[pl.ds(0, n - 1)], sems.at[0])
    wait_bytes(recv_buf.at[pl.ds(0, n - 1)], sems.at[2])
    wait_bytes(recv_buf.at[pl.ds(0, n - 1)], sems.at[4])
    wait_bytes(wz.at[pl.ds(0, blocks - 1)], sems.at[6])
    wait_bytes(wa.at[pl.ds(0, na - 1)], sems.at[8])
    wait_bytes(wy.at[pl.ds(0, n - 1)], sems.at[10])
    wait_bytes(wfin.at[pl.ds(0, na - 1)], sems.at[12])
    wait_bytes(wall.at[pl.ds(0, blocks - 1)], sems.at[14])


def body(features, tiles, weight, cotangent, send_count, send_index, cross_dst, cross_weight):
    rows, width = features.shape
    groups = lax.axis_size("comm")
    blocks = lax.axis_size("blk")
    slots = send_index.shape[1]
    cap = slots // groups
    na = groups // NY
    per = na * cap
    unit = rows // PARTS
    wrows = width // blocks
    piece = 2 * wrows // na
    half = width // 2
    vmem = pltpu.VMEM
    dma = pltpu.SemaphoreType.DMA
    return pl.pallas_call(
        functools.partial(kernel, groups, blocks),
        out_shape=(
            jax.ShapeDtypeStruct((rows, width), F32),
            jax.ShapeDtypeStruct((rows, width), F32),
            jax.ShapeDtypeStruct((width, width), F32),
        ),
        in_specs=[pl.BlockSpec(memory_space=pltpu.HBM)] * 8,
        out_specs=(pl.BlockSpec(memory_space=vmem),) * 3,
        scratch_shapes=[
            vmem(tiles.shape, F32), vmem(weight.shape, F32), vmem((rows, width), F32),
            vmem(send_count.shape, jnp.int32), vmem(send_index.shape, jnp.int32),
            vmem(cross_dst.shape, jnp.int32), vmem(cross_weight.shape, F32),
            vmem((2, NY * rows, width), F32),
            vmem((NY, rows, 2 * per), BF16),
            vmem((blocks, rows, 3 * rows), BF16), vmem((blocks, rows, 3 * rows), BF16),
            vmem((NY, rows, 3 * per), BF16), vmem((NY, per, 3 * rows), BF16),
            vmem((3 * width, width), BF16), vmem((3 * width, width), BF16),
            vmem((NY, 8, per), F32), vmem((NY, 8, per), F32),
            vmem((NY, per, width), F32), vmem((NY, per, width), F32),
            vmem((NY, per, width), F32), vmem((NY, per, width), F32),
            vmem((2, NY, rows, width), F32),
            vmem((4, UNITS, unit, width), F32), vmem((4, UNITS, unit, width), F32),
            vmem((width, width), F32),
            vmem((blocks, wrows, width), F32),
            vmem((na, piece, half), F32),
            vmem((NY, piece, half), F32),
            vmem((na, piece, half), F32),
            vmem((blocks, 2 * wrows, half), F32),
            vmem((2 * wrows, half), F32),
            dma((9,)), dma((4 * UNITS,)), dma((4,)), dma((4 * UNITS,)), dma((4,)), dma((NY,)), dma((NY,)), dma((16,)),
        ],
        compiler_params=pltpu.CompilerParams(
            collective_id=0, has_side_effects=True, vmem_limit_bytes=48 * 1024 * 1024
        ),
    )(*(pltpu.with_memory_space_constraint(v, pltpu.HBM) for v in (
        features, tiles, weight, cotangent, send_count, send_index, cross_dst, cross_weight)))


def solution(mesh):
    rows = P(("comm", "blk"), None)
    return jax.shard_map(
        body,
        mesh=mesh,
        in_specs=(rows, rows, P(), rows, rows, rows, rows, rows),
        out_specs=(rows, rows, P()),
        check_vma=False,
    )
```

```python
import functools

import jax
import jax.numpy as jnp
from jax import lax
from jax.experimental import pallas as pl
from jax.experimental.pallas import tpu as pltpu
from jax.sharding import PartitionSpec as P

MESH = pl.DeviceIdType.MESH
F32 = jnp.float32
BF16 = jnp.bfloat16
NY = 8
PARTS = 4
UNITS = 7 * PARTS // 2


def split(x):
    hi = x.astype(BF16)
    lo = (x - hi.astype(F32)).astype(BF16)
    return hi, lo


def mm(a, b, ca=1, cb=0):
    return lax.dot_general(a, b, (((ca,), (cb,)), ((), ())), preferred_element_type=F32)


def left(x, axis=1):
    return jnp.concatenate((x[0], x[0], x[1]), axis=axis)


def right(x):
    return jnp.concatenate((x[0], x[1], x[0]), axis=0)


def at(i, n):
    return pl.ds(pl.multiple_of(i * n, n), n)


def kernel(
    groups, blocks,
    f_hbm, t_hbm, w_hbm, ct_hbm, cnt_hbm, idx_hbm, dst_hbm, cw_hbm,
    all_ref,
    t_ref, w_ref, ct_ref, cnt_ref, idx_ref, dst_ref, cw_ref,
    gath, picks, t3, tt3, s3, st3, w3, wt3, idx_out, idx_in,
    send_buf, recv_buf, send2_buf, recv2_buf, part, rs_out, rs_in,
    wpart, wz, wa, wy, wfin, wall, wsum,
    loc, ag_r, ag_s, rs_r, rs_s, row_r, rowf_r, wfin_r, sems,
):
    rows, width = f_hbm.shape
    out_ref = all_ref.at[pl.ds(0, rows)]
    gf_ref = all_ref.at[pl.ds(rows, rows)]
    gw_ref = all_ref.at[pl.ds(2 * rows, width)]
    slots = idx_ref.shape[1]
    cap = slots // groups
    na = groups // NY
    unit = rows // PARTS
    me_c = lax.axis_index("comm")
    me_b = lax.axis_index("blk")
    core = lax.rem(me_c, 2)
    my_y = lax.rem(me_c // 2, NY)
    my_x = me_c // (2 * NY)
    my_a = my_x * 2 + core

    def a_dev(a):
        return (((a // 2) * NY + my_y) * 2 + lax.rem(a, 2), me_b)

    def y_dev(y):
        return ((my_x * NY + y) * 2 + core, me_b)

    def z_dev(z):
        return (me_c, z)

    ring = ((my_y, y_dev), (me_b, z_dev))
    n = NY

    def turn(r, d):
        return lax.rem(ring[r][0] + d + n, n)

    def send(src, dst, s, r, dev):
        pltpu.make_async_remote_copy(
            src_ref=src, dst_ref=dst, send_sem=s, recv_sem=r,
            device_id=dev, device_id_type=MESH,
        ).start()

    def wait_bytes(ref, s):
        pltpu.make_async_copy(ref, ref, s).wait()

    loads = [
        pltpu.make_async_copy(src, dst, loc.at[i])
        for i, (src, dst) in enumerate((
            (idx_hbm, idx_ref), (cnt_hbm, cnt_ref),
            (f_hbm, gath.at[0, at(my_y, rows)]), (f_hbm, gath.at[1, at(me_b, rows)]),
            (t_hbm, t_ref), (dst_hbm, dst_ref), (cw_hbm, cw_ref), (w_hbm, w_ref), (ct_hbm, ct_ref),
        ))
    ]
    for c in loads:
        c.start()

    barrier = pltpu.get_barrier_semaphore()

    @pl.loop(1, n)
    def _(i):
        pl.semaphore_signal(barrier, inc=1, device_id=y_dev(turn(0, i)), device_id_type=MESH)
        pl.semaphore_signal(barrier, inc=1, device_id=z_dev(turn(1, i)), device_id_type=MESH)
        pl.semaphore_signal(barrier, inc=1, device_id=a_dev(lax.rem(my_a + i, na)), device_id_type=MESH)

    loads[2].wait()
    loads[3].wait()

    pl.semaphore_wait(barrier, 3 * (n - 1))

    def part_of(sign, u):
        return (u % PARTS) if sign > 0 else (PARTS - 1 - u % PARTS)

    def ring_no(r, sign):
        return 2 * r + (0 if sign > 0 else 1)

    def ag_slice(r, sign, u, origin):
        return gath.at[r, pl.ds(pl.multiple_of(origin * rows + part_of(sign, u) * unit, unit), unit)]

    def ag_send(r, sign, u):
        s = ag_slice(r, sign, u, turn(r, -sign * (u // PARTS)))
        k = ring_no(r, sign)
        send(s, s, ag_s.at[k], ag_r.at[k * UNITS + u], ring[r][1](turn(r, sign)))

    def ag_wait(r, sign, u):
        s = ag_slice(r, sign, u, turn(r, -sign * (u // PARTS + 1)))
        wait_bytes(s, ag_r.at[ring_no(r, sign) * UNITS + u])

    for u in range(PARTS):
        for r in (0, 1):
            for sign in (1, -1):
                ag_send(r, sign, u)

    per = na * cap
    spot = lax.broadcasted_iota(jnp.int32, (groups, slots), 1) // cap
    peer = lax.broadcasted_iota(jnp.int32, (groups, slots), 0)
    expand = (spot == peer).astype(BF16)
    lane = lax.broadcasted_iota(jnp.int32, (16, slots), 1)
    row16 = lax.broadcasted_iota(jnp.int32, (16, slots), 0)
    here = (lane // (2 * cap)) % NY == row16
    source = lax.broadcasted_iota(jnp.int32, (slots, per), 0)
    target = lax.broadcasted_iota(jnp.int32, (slots, per), 1)
    gather_lane = ((source // (2 * cap * NY)) * (2 * cap) + source % (2 * cap) == target).astype(BF16)
    place = lax.rem(lane, cap).astype(F32)

    def by_y(v):
        v = jnp.broadcast_to(v, (16, slots)).astype(F32)
        return mm(jnp.where(here, v, 0.0).astype(BF16), gather_lane)

    loads[0].wait()
    loads[1].wait()
    counts = jnp.broadcast_to(cnt_ref[...].astype(F32).astype(BF16), (16, groups))
    count = mm(counts, expand)
    index = jnp.where(place < count, jnp.broadcast_to(idx_ref[...], (16, slots)).astype(F32), -1.0)
    mine = by_y(index)
    for y in range(NY):
        idx_out[y] = jnp.broadcast_to(mine[y:y + 1, :], (8, per))
    idx_in[my_y] = idx_out[my_y]

    @pl.loop(1, n)
    def _(i):
        y = turn(0, i)
        send(idx_out.at[y], idx_in.at[my_y], sems.at[0], sems.at[1], y_dev(y))

    node = lax.broadcasted_iota(jnp.int32, (rows, per), 0).astype(F32)

    def pick_block(y):
        pick = (node == idx_in[y][0:1, :]).astype(F32)
        one = pick.astype(BF16)
        picks[y] = jnp.concatenate((one, one), axis=1)
        flip = pick.T.astype(BF16)
        g = split(gath[0, at(y, rows), :])
        send_buf[y] = mm(jnp.concatenate((flip, flip), axis=1), jnp.concatenate(g, axis=0))

        @pl.loop(1, na)
        def _(i):
            a = lax.rem(my_a + i, na)
            send(send_buf.at[y, at(a, cap)], recv_buf.at[y, at(my_a, cap)], sems.at[2], rowf_r.at[y], a_dev(a))

        recv_buf[y, at(my_a, cap), :] = send_buf[y, at(my_a, cap), :]

    def make_tiles(js):
        for j in js:
            v = t_ref[:, j * rows:(j + 1) * rows]
            t3[j] = left(split(v))
            tt3[j] = left(split(v.T))

    def cross_wait(y):
        wait_bytes(recv_buf.at[y, pl.ds(0, cap * (na - 1))], rowf_r.at[y])

    def gathered(ref, blocks_of, data):
        a = jnp.concatenate([ref[b] for b in blocks_of], axis=1)
        return mm(a, jnp.concatenate([right(split(data(b))) for b in blocks_of], axis=0))

    def local_blocks(*js):
        return gathered(t3, js, lambda j: gath[1, at(j, rows), :])

    def cross_blocks(*ys):
        for y in ys:
            cross_wait(y)
        return gathered(s3, ys, lambda y: recv_buf[y])

    def ring_step(k):
        for u in range(k * PARTS // 2, (k + 1) * PARTS // 2):
            for r in (0, 1):
                for sign in (1, -1):
                    ag_wait(r, sign, u)
                    if u + PARTS < UNITS:
                        ag_send(r, sign, u + PARTS)

    pick_block(my_y)
    ring_step(0)
    for c in loads[4:]:
        c.wait()
    make_tiles(range(blocks))
    wait_bytes(idx_in.at[pl.ds(0, n - 1)], sems.at[1])
    ring_step(1)
    pick_block(turn(0, 1))
    pick_block(turn(0, -1))
    ring_step(2)
    feed = by_y(dst_ref[...])
    cw2 = split(cw_ref[...])
    weight_hi = by_y(cw2[0].astype(F32))
    weight_lo = by_y(cw2[1].astype(F32))
    for y in range(NY):
        hit = node == feed[y:y + 1, :]
        hi = jnp.where(hit, jnp.broadcast_to(weight_hi[y:y + 1, :], (rows, per)), 0.0)
        lo = jnp.where(hit, jnp.broadcast_to(weight_lo[y:y + 1, :], (rows, per)), 0.0)
        s3[y] = left((hi.astype(BF16), lo.astype(BF16)))
        st3[y] = left((hi.T.astype(BF16), lo.T.astype(BF16)))
    ring_step(3)
    pick_block(turn(0, 2))
    pick_block(turn(0, -2))
    ring_step(4)
    w3[...] = right(split(w_ref[...]))
    wt3[...] = right(split(w_ref[...].T))
    agg = local_blocks(me_b, turn(1, 1), turn(1, -1))
    ring_step(5)
    pick_block(turn(0, 3))
    pick_block(turn(0, -3))
    ring_step(6)
    pick_block(turn(0, 4))
    agg = agg + local_blocks(turn(1, 2), turn(1, -2))
    agg = agg + local_blocks(turn(1, 3), turn(1, -3), turn(1, 4))
    agg = agg + cross_blocks(my_y, turn(0, 1), turn(0, -1))
    agg = agg + cross_blocks(turn(0, 2), turn(0, -2))
    agg = agg + cross_blocks(turn(0, 3), turn(0, -3), turn(0, 4))
    agg2 = split(agg)
    pre = mm(left(agg2), w3[...])
    cdf = 0.5 * (1.0 + lax.erf(pre * 0.7071067811865476))
    out_ref[...] = pre * cdf
    slope = cdf + pre * (jnp.exp(-0.5 * pre * pre) * 0.3989422804014327)
    gp2 = split(ct_ref[...] * slope)

    sp3 = right(split(mm(left(gp2), wt3[...])))

    def give_back(y):
        send2_buf[y] = mm(st3[y], sp3)

        @pl.loop(1, na)
        def _(i):
            a = lax.rem(my_a + i, na)
            send(send2_buf.at[y, at(a, cap)], recv2_buf.at[y, at(my_a, cap)], sems.at[4], row_r.at[y], a_dev(a))

        recv2_buf[y, at(my_a, cap), :] = send2_buf[y, at(my_a, cap), :]

    def inner_block(j):
        part[1, j] = mm(tt3[j], sp3)

    def boundary_block(y):
        wait_bytes(recv2_buf.at[y, pl.ds(0, cap * (na - 1))], row_r.at[y])
        part[0, y] = mm(picks[y], jnp.concatenate(split(recv2_buf[y]), axis=0))

    def rs_step(r, sign, u):
        k = ring_no(r, sign)
        owner = turn(r, sign * (4 - (u + PARTS // 2) // PARTS))
        h = part_of(sign, u) * unit
        v = part[r, owner, h:h + unit, :]
        if u >= PARTS:
            wait_bytes(rs_in.at[k, u - PARTS], rs_r.at[k * UNITS + u - PARTS])
            v = v + rs_in[k, u - PARTS]
        rs_out[k, u] = v
        send(rs_out.at[k, u], rs_in.at[k, u], rs_s.at[k], rs_r.at[k * UNITS + u], ring[r][1](turn(r, sign)))

    def rs_all(r, k):
        for u in range(k * PARTS // 2, (k + 1) * PARTS // 2):
            rs_step(r, 1, u)
            rs_step(r, -1, u)

    wrows = width // na
    half = width // 2
    piece = 2 * wrows // n

    def weight_1():
        wpart[...] = mm(left(agg2, 0), right(gp2), 0, 0)

        @pl.loop(1, na)
        def _(i):
            a = lax.rem(my_a + i, na)
            send(wpart.at[at(a, wrows)], wz.at[my_a], sems.at[6], sems.at[7], a_dev(a))

        wz[my_a] = wpart[at(my_a, wrows), :]

    def weight_2():
        wait_bytes(wz.at[pl.ds(0, na - 1)], sems.at[7])
        total = jnp.sum(wz[...], axis=0)
        wsum[0:wrows, :] = total[:, :half]
        wsum[wrows:, :] = total[:, half:]

        @pl.loop(1, n)
        def _(i):
            y = turn(0, i)
            send(wsum.at[at(y, piece)], wa.at[my_y], sems.at[8], sems.at[9], y_dev(y))

        wa[my_y] = wsum[at(my_y, piece), :]

    def weight_3():
        wait_bytes(wa.at[pl.ds(0, n - 1)], sems.at[9])
        wy[me_b] = jnp.sum(wa[...], axis=0)

        @pl.loop(1, n)
        def _(i):
            send(wy.at[me_b], wy.at[me_b], sems.at[10], sems.at[11], z_dev(turn(1, i)))

    def weight_4():
        wait_bytes(wy.at[pl.ds(0, n - 1)], sems.at[11])
        nodes = rows * groups * blocks
        wfin[my_y] = jnp.sum(wy[...], axis=0) * nodes ** (-0.5)

        @pl.loop(1, n)
        def _(i):
            send(wfin.at[my_y], wfin.at[my_y], sems.at[12], wfin_r.at[my_y], y_dev(turn(0, i)))

    def weight_5():
        for d in (0, 1, -1, 2, -2, 3, -3, 4):
            y = turn(0, d)
            if d:
                wait_bytes(wfin.at[y], wfin_r.at[y])

            @pl.loop(1, na)
            def _(i):
                send(wfin.at[y], wall.at[my_a, y], sems.at[14], sems.at[15], a_dev(lax.rem(my_a + i, na)))

        wall[my_a] = wfin[...]

    weight_1()
    inner_block(turn(1, 4))
    rs_all(1, 0)
    inner_block(turn(1, 3))
    inner_block(turn(1, -3))
    rs_all(1, 1)
    for d in (4, 3, -3, 2, -2, 1, -1, 0):
        give_back(turn(0, d))
    inner_block(turn(1, 2))
    inner_block(turn(1, -2))
    rs_all(1, 2)
    weight_2()
    boundary_block(turn(0, 4))
    rs_all(0, 0)
    boundary_block(turn(0, 3))
    boundary_block(turn(0, -3))
    rs_all(0, 1)
    rs_all(1, 3)
    inner_block(turn(1, 1))
    inner_block(turn(1, -1))
    weight_3()
    rs_all(1, 4)
    rs_all(0, 2)
    boundary_block(turn(0, 2))
    boundary_block(turn(0, -2))
    rs_all(0, 3)
    weight_4()
    rs_all(1, 5)
    rs_all(0, 4)
    boundary_block(turn(0, 1))
    boundary_block(turn(0, -1))
    rs_all(0, 5)
    rs_all(1, 6)
    weight_5()
    rs_all(0, 6)
    inner_block(me_b)
    boundary_block(my_y)

    last = range(UNITS - PARTS, UNITS)
    for k in range(4):
        for u in last:
            wait_bytes(rs_in.at[k, u], rs_r.at[k * UNITS + u])
    for h in range(PARTS):
        at_h = slice(h * unit, (h + 1) * unit)
        own = part[0, my_y, at_h, :] + part[1, me_b, at_h, :]
        for r in (0, 1):
            for sign in (1, -1):
                for u in last:
                    if part_of(sign, u) == h:
                        own = own + rs_in[ring_no(r, sign), u]
        gf_ref[at_h, :] = own

    wait_bytes(wall.at[pl.ds(0, na - 1)], sems.at[15])
    for j in range(na):
        gw_ref[j * wrows:(j + 1) * wrows, :half] = wall[j, 0:n // 2].reshape(wrows, half)
        gw_ref[j * wrows:(j + 1) * wrows, half:] = wall[j, n // 2:].reshape(wrows, half)

    for k in range(4):
        wait_bytes(gath.at[0, pl.ds(0, UNITS * unit)], ag_s.at[k])
        wait_bytes(rs_out.at[k], rs_s.at[k])
    wait_bytes(idx_out.at[pl.ds(0, n - 1)], sems.at[0])
    wait_bytes(recv_buf.at[pl.ds(0, n - 1)], sems.at[2])
    wait_bytes(recv_buf.at[pl.ds(0, n - 1)], sems.at[4])
    wait_bytes(wz.at[pl.ds(0, blocks - 1)], sems.at[6])
    wait_bytes(wa.at[pl.ds(0, na - 1)], sems.at[8])
    wait_bytes(wy.at[pl.ds(0, n - 1)], sems.at[10])
    wait_bytes(wfin.at[pl.ds(0, na - 1)], sems.at[12])
    wait_bytes(wall.at[pl.ds(0, na - 1)], sems.at[14])


def body(features, tiles, weight, cotangent, send_count, send_index, cross_dst, cross_weight):
    rows, width = features.shape
    groups = lax.axis_size("comm")
    blocks = lax.axis_size("blk")
    slots = send_index.shape[1]
    cap = slots // groups
    na = groups // NY
    per = na * cap
    unit = rows // PARTS
    wrows = width // blocks
    piece = 2 * wrows // na
    half = width // 2
    vmem = pltpu.VMEM
    dma = pltpu.SemaphoreType.DMA
    full = pl.pallas_call(
        functools.partial(kernel, groups, blocks),
        out_shape=jax.ShapeDtypeStruct((2 * rows + width, width), F32),
        in_specs=[pl.BlockSpec(memory_space=pltpu.HBM)] * 8,
        out_specs=pl.BlockSpec(memory_space=vmem),
        scratch_shapes=[
            vmem(tiles.shape, F32), vmem(weight.shape, F32), vmem((rows, width), F32),
            vmem(send_count.shape, jnp.int32), vmem(send_index.shape, jnp.int32),
            vmem(cross_dst.shape, jnp.int32), vmem(cross_weight.shape, F32),
            vmem((2, NY * rows, width), F32),
            vmem((NY, rows, 2 * per), BF16),
            vmem((blocks, rows, 3 * rows), BF16), vmem((blocks, rows, 3 * rows), BF16),
            vmem((NY, rows, 3 * per), BF16), vmem((NY, per, 3 * rows), BF16),
            vmem((3 * width, width), BF16), vmem((3 * width, width), BF16),
            vmem((NY, 8, per), F32), vmem((NY, 8, per), F32),
            vmem((NY, per, width), F32), vmem((NY, per, width), F32),
            vmem((NY, per, width), F32), vmem((NY, per, width), F32),
            vmem((2, NY, rows, width), F32),
            vmem((4, UNITS, unit, width), F32), vmem((4, UNITS, unit, width), F32),
            vmem((width, width), F32),
            vmem((blocks, wrows, width), F32),
            vmem((na, piece, half), F32),
            vmem((NY, piece, half), F32),
            vmem((na, piece, half), F32),
            vmem((na, NY, piece, half), F32),
            vmem((2 * wrows, half), F32),
            dma((9,)), dma((4 * UNITS,)), dma((4,)), dma((4 * UNITS,)), dma((4,)), dma((NY,)), dma((NY,)), dma((NY,)), dma((16,)),
        ],
        compiler_params=pltpu.CompilerParams(
            collective_id=0, has_side_effects=True, vmem_limit_bytes=48 * 1024 * 1024
        ),
    )(*(pltpu.with_memory_space_constraint(v, pltpu.HBM) for v in (
        features, tiles, weight, cotangent, send_count, send_index, cross_dst, cross_weight)))

    return full[:rows], full[rows:2 * rows], full[2 * rows:]


def solution(mesh):
    rows = P(("comm", "blk"), None)
    return jax.shard_map(
        body,
        mesh=mesh,
        in_specs=(rows, rows, P(), rows, rows, rows, rows, rows),
        out_specs=(rows, rows, P()),
        check_vma=False,
    )
```

```python
import functools

import jax
import jax.numpy as jnp
from jax import lax
from jax.experimental import pallas as pl
from jax.experimental.pallas import tpu as pltpu
from jax.sharding import PartitionSpec as P

MESH = pl.DeviceIdType.MESH
F32 = jnp.float32
BF16 = jnp.bfloat16
NY = 8
PARTS = 2
UNITS = 7 * PARTS // 2


def split(x):
    hi = x.astype(BF16)
    lo = (x - hi.astype(F32)).astype(BF16)
    return hi, lo


def mm(a, b, ca=1, cb=0):
    return lax.dot_general(a, b, (((ca,), (cb,)), ((), ())), preferred_element_type=F32)


def left(x, axis=1):
    return jnp.concatenate((x[0], x[0], x[1]), axis=axis)


def right(x):
    return jnp.concatenate((x[0], x[1], x[0]), axis=0)


def at(i, n):
    return pl.ds(pl.multiple_of(i * n, n), n)


def kernel(
    groups, blocks,
    f_hbm, t_hbm, w_hbm, ct_hbm, cnt_hbm, idx_hbm, dst_hbm, cw_hbm,
    all_ref,
    t_ref, w_ref, ct_ref, cnt_ref, idx_ref, dst_ref, cw_ref,
    gath, picks, flips, t3, tt3, s3, st3, w3, wt3, idx_out, idx_in,
    send_buf, recv_buf, send2_buf, recv2_buf, part, rs_out, rs_in,
    wpart, wz, wa, wy, wfin, wall, wsum,
    loc, ag_r, ag_s, rs_r, rs_s, row_r, rowf_r, wfin_r, sems,
):
    rows, width = f_hbm.shape
    out_ref = all_ref.at[pl.ds(0, rows)]
    gf_ref = all_ref.at[pl.ds(rows, rows)]
    gw_ref = all_ref.at[pl.ds(2 * rows, width)]
    slots = idx_ref.shape[1]
    cap = slots // groups
    na = groups // NY
    unit = rows // PARTS
    me_c = lax.axis_index("comm")
    me_b = lax.axis_index("blk")
    core = lax.rem(me_c, 2)
    my_y = lax.rem(me_c // 2, NY)
    my_x = me_c // (2 * NY)
    my_a = my_x * 2 + core

    def a_dev(a):
        return (((a // 2) * NY + my_y) * 2 + lax.rem(a, 2), me_b)

    def y_dev(y):
        return ((my_x * NY + y) * 2 + core, me_b)

    def z_dev(z):
        return (me_c, z)

    ring = ((my_y, y_dev), (me_b, z_dev))
    n = NY

    def turn(r, d):
        return lax.rem(ring[r][0] + d + n, n)

    def send(src, dst, s, r, dev):
        pltpu.make_async_remote_copy(
            src_ref=src, dst_ref=dst, send_sem=s, recv_sem=r,
            device_id=dev, device_id_type=MESH,
        ).start()

    def wait_bytes(ref, s):
        pltpu.make_async_copy(ref, ref, s).wait()

    loads = [
        pltpu.make_async_copy(src, dst, loc.at[i])
        for i, (src, dst) in enumerate((
            (idx_hbm, idx_ref), (cnt_hbm, cnt_ref),
            (f_hbm, gath.at[0, at(my_y, rows)]), (f_hbm, gath.at[1, at(me_b, rows)]),
            (t_hbm, t_ref), (dst_hbm, dst_ref), (cw_hbm, cw_ref), (w_hbm, w_ref), (ct_hbm, ct_ref),
        ))
    ]
    for c in loads:
        c.start()

    barrier = pltpu.get_barrier_semaphore()

    @pl.loop(1, n)
    def _(i):
        pl.semaphore_signal(barrier, inc=1, device_id=y_dev(turn(0, i)), device_id_type=MESH)
        pl.semaphore_signal(barrier, inc=1, device_id=z_dev(turn(1, i)), device_id_type=MESH)
        pl.semaphore_signal(barrier, inc=1, device_id=a_dev(lax.rem(my_a + i, na)), device_id_type=MESH)

    loads[2].wait()
    loads[3].wait()

    pl.semaphore_wait(barrier, 3 * (n - 1))

    def part_of(sign, u):
        return (u % PARTS) if sign > 0 else (PARTS - 1 - u % PARTS)

    def ring_no(r, sign):
        return 2 * r + (0 if sign > 0 else 1)

    def ag_slice(r, sign, u, origin):
        return gath.at[r, pl.ds(pl.multiple_of(origin * rows + part_of(sign, u) * unit, unit), unit)]

    def ag_send(r, sign, u):
        s = ag_slice(r, sign, u, turn(r, -sign * (u // PARTS)))
        k = ring_no(r, sign)
        send(s, s, ag_s.at[k], ag_r.at[k * UNITS + u], ring[r][1](turn(r, sign)))

    def ag_wait(r, sign, u):
        s = ag_slice(r, sign, u, turn(r, -sign * (u // PARTS + 1)))
        wait_bytes(s, ag_r.at[ring_no(r, sign) * UNITS + u])

    for u in range(PARTS):
        for r in (0, 1):
            for sign in (1, -1):
                ag_send(r, sign, u)

    per = na * cap
    spot = lax.broadcasted_iota(jnp.int32, (groups, slots), 1) // cap
    peer = lax.broadcasted_iota(jnp.int32, (groups, slots), 0)
    expand = (spot == peer).astype(BF16)
    lane = lax.broadcasted_iota(jnp.int32, (16, slots), 1)
    row16 = lax.broadcasted_iota(jnp.int32, (16, slots), 0)
    here = (lane // (2 * cap)) % NY == row16
    source = lax.broadcasted_iota(jnp.int32, (slots, per), 0)
    target = lax.broadcasted_iota(jnp.int32, (slots, per), 1)
    gather_lane = ((source // (2 * cap * NY)) * (2 * cap) + source % (2 * cap) == target).astype(BF16)
    place = lax.rem(lane, cap).astype(F32)

    def by_y(v):
        v = jnp.broadcast_to(v, (16, slots)).astype(F32)
        return mm(jnp.where(here, v, 0.0).astype(BF16), gather_lane)

    loads[0].wait()
    loads[1].wait()
    counts = jnp.broadcast_to(cnt_ref[...].astype(F32).astype(BF16), (16, groups))
    count = mm(counts, expand)
    index = jnp.where(place < count, jnp.broadcast_to(idx_ref[...], (16, slots)).astype(F32), -1.0)
    mine = by_y(index)
    for y in range(NY):
        idx_out[y] = jnp.broadcast_to(mine[y:y + 1, :], (8, per))
    idx_in[my_y] = idx_out[my_y]

    @pl.loop(1, n)
    def _(i):
        y = turn(0, i)
        send(idx_out.at[y], idx_in.at[my_y], sems.at[0], sems.at[1], y_dev(y))

    node = lax.broadcasted_iota(jnp.int32, (rows, per), 0).astype(F32)

    def make_pick(y):
        pick = (node == idx_in[y][0:1, :]).astype(F32)
        one = pick.astype(BF16)
        picks[y] = jnp.concatenate((one, one), axis=1)
        flip = pick.T.astype(BF16)
        flips[y] = jnp.concatenate((flip, flip), axis=1)

    def pick_block(y):
        g = split(gath[0, at(y, rows), :])
        send_buf[y] = mm(flips[y], jnp.concatenate(g, axis=0))

        @pl.loop(1, na)
        def _(i):
            a = lax.rem(my_a + i, na)
            send(send_buf.at[y, at(a, cap)], recv_buf.at[y, at(my_a, cap)], sems.at[2], rowf_r.at[y], a_dev(a))

        recv_buf[y, at(my_a, cap), :] = send_buf[y, at(my_a, cap), :]

    def make_tiles(js):
        for j in js:
            v = t_ref[:, j * rows:(j + 1) * rows]
            t3[j] = left(split(v))
            tt3[j] = left(split(v.T))

    def cross_wait(y):
        wait_bytes(recv_buf.at[y, pl.ds(0, cap * (na - 1))], rowf_r.at[y])

    def gathered(ref, blocks_of, data):
        a = jnp.concatenate([ref[b] for b in blocks_of], axis=1)
        return mm(a, jnp.concatenate([right(split(data(b))) for b in blocks_of], axis=0))

    def local_blocks(*js):
        return gathered(t3, js, lambda j: gath[1, at(j, rows), :])

    def cross_blocks(*ys):
        for y in ys:
            cross_wait(y)
        return gathered(s3, ys, lambda y: recv_buf[y])

    def ring_step(r, k):
        for u in range(k * PARTS // 2, (k + 1) * PARTS // 2):
            for sign in (1, -1):
                ag_wait(r, sign, u)
                if u + PARTS < UNITS:
                    ag_send(r, sign, u + PARTS)

    make_pick(my_y)
    pick_block(my_y)
    ring_step(0, 0)
    ring_step(1, 0)
    for c in loads[4:]:
        c.wait()
    make_tiles(range(blocks))
    wait_bytes(idx_in.at[pl.ds(0, n - 1)], sems.at[1])
    for d in (1, -1):
        make_pick(turn(0, d))
    ring_step(0, 1)
    pick_block(turn(0, 1))
    pick_block(turn(0, -1))
    ring_step(1, 1)
    for d in (2, -2, 3, -3, 4):
        make_pick(turn(0, d))
    ring_step(0, 2)
    ring_step(1, 2)
    feed = by_y(dst_ref[...])
    cw2 = split(cw_ref[...])
    weight_hi = by_y(cw2[0].astype(F32))
    weight_lo = by_y(cw2[1].astype(F32))
    for y in range(NY):
        hit = node == feed[y:y + 1, :]
        hi = jnp.where(hit, jnp.broadcast_to(weight_hi[y:y + 1, :], (rows, per)), 0.0)
        lo = jnp.where(hit, jnp.broadcast_to(weight_lo[y:y + 1, :], (rows, per)), 0.0)
        s3[y] = left((hi.astype(BF16), lo.astype(BF16)))
        st3[y] = left((hi.T.astype(BF16), lo.T.astype(BF16)))
    ring_step(0, 3)
    pick_block(turn(0, 2))
    pick_block(turn(0, -2))
    ring_step(1, 3)
    ring_step(0, 4)
    ring_step(1, 4)
    w3[...] = right(split(w_ref[...]))
    wt3[...] = right(split(w_ref[...].T))
    agg = local_blocks(me_b, turn(1, 1), turn(1, -1))
    ring_step(0, 5)
    pick_block(turn(0, 3))
    pick_block(turn(0, -3))
    ring_step(1, 5)
    ring_step(0, 6)
    pick_block(turn(0, 4))
    ring_step(1, 6)
    agg = agg + local_blocks(turn(1, 2), turn(1, -2))
    agg = agg + local_blocks(turn(1, 3), turn(1, -3), turn(1, 4))
    agg = agg + cross_blocks(my_y, turn(0, 1), turn(0, -1))
    agg = agg + cross_blocks(turn(0, 2), turn(0, -2))
    agg = agg + cross_blocks(turn(0, 3), turn(0, -3), turn(0, 4))
    agg2 = split(agg)
    pre = mm(left(agg2), w3[...])
    cdf = 0.5 * (1.0 + lax.erf(pre * 0.7071067811865476))
    out_ref[...] = pre * cdf
    slope = cdf + pre * (jnp.exp(-0.5 * pre * pre) * 0.3989422804014327)
    gp2 = split(ct_ref[...] * slope)

    sp3 = right(split(mm(left(gp2), wt3[...])))

    def give_back(y):
        send2_buf[y] = mm(st3[y], sp3)

        @pl.loop(1, na)
        def _(i):
            a = lax.rem(my_a + i, na)
            send(send2_buf.at[y, at(a, cap)], recv2_buf.at[y, at(my_a, cap)], sems.at[4], row_r.at[y], a_dev(a))

        recv2_buf[y, at(my_a, cap), :] = send2_buf[y, at(my_a, cap), :]

    def inner_block(j):
        part[1, j] = mm(tt3[j], sp3)

    def boundary_block(y):
        wait_bytes(recv2_buf.at[y, pl.ds(0, cap * (na - 1))], row_r.at[y])
        part[0, y] = mm(picks[y], jnp.concatenate(split(recv2_buf[y]), axis=0))

    def rs_step(r, sign, u):
        k = ring_no(r, sign)
        owner = turn(r, sign * (4 - (u + PARTS // 2) // PARTS))
        h = part_of(sign, u) * unit
        v = part[r, owner, h:h + unit, :]
        if u >= PARTS:
            wait_bytes(rs_in.at[k, u - PARTS], rs_r.at[k * UNITS + u - PARTS])
            v = v + rs_in[k, u - PARTS]
        rs_out[k, u] = v
        send(rs_out.at[k, u], rs_in.at[k, u], rs_s.at[k], rs_r.at[k * UNITS + u], ring[r][1](turn(r, sign)))

    def rs_all(r, k):
        for u in range(k * PARTS // 2, (k + 1) * PARTS // 2):
            rs_step(r, 1, u)
            rs_step(r, -1, u)

    wrows = width // na
    half = width // 2
    piece = 2 * wrows // n

    def weight_1():
        wpart[...] = mm(left(agg2, 0), right(gp2), 0, 0)

        @pl.loop(1, na)
        def _(i):
            a = lax.rem(my_a + i, na)
            send(wpart.at[at(a, wrows)], wz.at[my_a], sems.at[6], sems.at[7], a_dev(a))

        wz[my_a] = wpart[at(my_a, wrows), :]

    def weight_2():
        wait_bytes(wz.at[pl.ds(0, na - 1)], sems.at[7])
        total = jnp.sum(wz[...], axis=0)
        wsum[0:wrows, :] = total[:, :half]
        wsum[wrows:, :] = total[:, half:]

        @pl.loop(1, n)
        def _(i):
            y = turn(0, i)
            send(wsum.at[at(y, piece)], wa.at[my_y], sems.at[8], sems.at[9], y_dev(y))

        wa[my_y] = wsum[at(my_y, piece), :]

    def weight_3():
        wait_bytes(wa.at[pl.ds(0, n - 1)], sems.at[9])
        wy[me_b] = jnp.sum(wa[...], axis=0)

        @pl.loop(1, n)
        def _(i):
            send(wy.at[me_b], wy.at[me_b], sems.at[10], sems.at[11], z_dev(turn(1, i)))

    def weight_4():
        wait_bytes(wy.at[pl.ds(0, n - 1)], sems.at[11])
        nodes = rows * groups * blocks
        wfin[my_y] = jnp.sum(wy[...], axis=0) * nodes ** (-0.5)

        @pl.loop(1, n)
        def _(i):
            send(wfin.at[my_y], wfin.at[my_y], sems.at[12], wfin_r.at[my_y], y_dev(turn(0, i)))

    def weight_5():
        for d in (0, 1, -1, 2, -2, 3, -3, 4):
            y = turn(0, d)
            if d:
                wait_bytes(wfin.at[y], wfin_r.at[y])

            @pl.loop(1, na)
            def _(i):
                send(wfin.at[y], wall.at[my_a, y], sems.at[14], sems.at[15], a_dev(lax.rem(my_a + i, na)))

        wall[my_a] = wfin[...]

    weight_1()
    inner_block(turn(1, 4))
    rs_all(1, 0)
    inner_block(turn(1, 3))
    inner_block(turn(1, -3))
    rs_all(1, 1)
    for d in (4, 3, -3, 2, -2, 1, -1, 0):
        give_back(turn(0, d))
    inner_block(turn(1, 2))
    inner_block(turn(1, -2))
    rs_all(1, 2)
    weight_2()
    boundary_block(turn(0, 4))
    rs_all(0, 0)
    boundary_block(turn(0, 3))
    boundary_block(turn(0, -3))
    rs_all(0, 1)
    rs_all(1, 3)
    inner_block(turn(1, 1))
    inner_block(turn(1, -1))
    rs_all(0, 2)
    weight_3()
    rs_all(1, 4)
    boundary_block(turn(0, 2))
    boundary_block(turn(0, -2))
    rs_all(0, 3)
    weight_4()
    rs_all(1, 5)
    rs_all(0, 4)
    boundary_block(turn(0, 1))
    boundary_block(turn(0, -1))
    rs_all(0, 5)
    rs_all(1, 6)
    weight_5()
    rs_all(0, 6)
    inner_block(me_b)
    boundary_block(my_y)

    last = range(UNITS - PARTS, UNITS)
    for k in range(4):
        for u in last:
            wait_bytes(rs_in.at[k, u], rs_r.at[k * UNITS + u])
    for h in range(PARTS):
        at_h = slice(h * unit, (h + 1) * unit)
        own = part[0, my_y, at_h, :] + part[1, me_b, at_h, :]
        for r in (0, 1):
            for sign in (1, -1):
                for u in last:
                    if part_of(sign, u) == h:
                        own = own + rs_in[ring_no(r, sign), u]
        gf_ref[at_h, :] = own

    wait_bytes(wall.at[pl.ds(0, na - 1)], sems.at[15])
    for j in range(na):
        gw_ref[j * wrows:(j + 1) * wrows, :half] = wall[j, 0:n // 2].reshape(wrows, half)
        gw_ref[j * wrows:(j + 1) * wrows, half:] = wall[j, n // 2:].reshape(wrows, half)

    for k in range(4):
        wait_bytes(gath.at[0, pl.ds(0, UNITS * unit)], ag_s.at[k])
        wait_bytes(rs_out.at[k], rs_s.at[k])
    wait_bytes(idx_out.at[pl.ds(0, n - 1)], sems.at[0])
    wait_bytes(recv_buf.at[pl.ds(0, n - 1)], sems.at[2])
    wait_bytes(recv_buf.at[pl.ds(0, n - 1)], sems.at[4])
    wait_bytes(wz.at[pl.ds(0, blocks - 1)], sems.at[6])
    wait_bytes(wa.at[pl.ds(0, na - 1)], sems.at[8])
    wait_bytes(wy.at[pl.ds(0, n - 1)], sems.at[10])
    wait_bytes(wfin.at[pl.ds(0, na - 1)], sems.at[12])
    wait_bytes(wall.at[pl.ds(0, na - 1)], sems.at[14])


def body(features, tiles, weight, cotangent, send_count, send_index, cross_dst, cross_weight):
    rows, width = features.shape
    groups = lax.axis_size("comm")
    blocks = lax.axis_size("blk")
    slots = send_index.shape[1]
    cap = slots // groups
    na = groups // NY
    per = na * cap
    unit = rows // PARTS
    wrows = width // blocks
    piece = 2 * wrows // na
    half = width // 2
    vmem = pltpu.VMEM
    dma = pltpu.SemaphoreType.DMA
    full = pl.pallas_call(
        functools.partial(kernel, groups, blocks),
        out_shape=jax.ShapeDtypeStruct((2 * rows + width, width), F32),
        in_specs=[pl.BlockSpec(memory_space=pltpu.HBM)] * 8,
        out_specs=pl.BlockSpec(memory_space=vmem),
        scratch_shapes=[
            vmem(tiles.shape, F32), vmem(weight.shape, F32), vmem((rows, width), F32),
            vmem(send_count.shape, jnp.int32), vmem(send_index.shape, jnp.int32),
            vmem(cross_dst.shape, jnp.int32), vmem(cross_weight.shape, F32),
            vmem((2, NY * rows, width), F32),
            vmem((NY, rows, 2 * per), BF16), vmem((NY, per, 2 * rows), BF16),
            vmem((blocks, rows, 3 * rows), BF16), vmem((blocks, rows, 3 * rows), BF16),
            vmem((NY, rows, 3 * per), BF16), vmem((NY, per, 3 * rows), BF16),
            vmem((3 * width, width), BF16), vmem((3 * width, width), BF16),
            vmem((NY, 8, per), F32), vmem((NY, 8, per), F32),
            vmem((NY, per, width), F32), vmem((NY, per, width), F32),
            vmem((NY, per, width), F32), vmem((NY, per, width), F32),
            vmem((2, NY, rows, width), F32),
            vmem((4, UNITS, unit, width), F32), vmem((4, UNITS, unit, width), F32),
            vmem((width, width), F32),
            vmem((blocks, wrows, width), F32),
            vmem((na, piece, half), F32),
            vmem((NY, piece, half), F32),
            vmem((na, piece, half), F32),
            vmem((na, NY, piece, half), F32),
            vmem((2 * wrows, half), F32),
            dma((9,)), dma((4 * UNITS,)), dma((4,)), dma((4 * UNITS,)), dma((4,)), dma((NY,)), dma((NY,)), dma((NY,)), dma((16,)),
        ],
        compiler_params=pltpu.CompilerParams(
            collective_id=0, has_side_effects=True, vmem_limit_bytes=48 * 1024 * 1024
        ),
    )(*(pltpu.with_memory_space_constraint(v, pltpu.HBM) for v in (
        features, tiles, weight, cotangent, send_count, send_index, cross_dst, cross_weight)))

    return full[:rows], full[rows:2 * rows], full[2 * rows:]


def solution(mesh):
    rows = P(("comm", "blk"), None)
    return jax.shard_map(
        body,
        mesh=mesh,
        in_specs=(rows, rows, P(), rows, rows, rows, rows, rows),
        out_specs=(rows, rows, P()),
        check_vma=False,
    )
```
